32 devices in a mesh: gx: 4 (over z), gy: 2 (over y), gz: 4 (over x, core).
Axes of the slice: x: 2, y: 2, z: 4, core: 2. Of those that a mesh axis runs over, the one named last changes fastest.
Arguments:
- points: float32 [1024, 3, 128], P(('gx', 'gy', 'gz'))
- charges: float32 [1024, 128], P(('gx', 'gy', 'gz')), may hold values from -0.6 to 0.6
- interpolant: float32 [1024, 64, 64], P(('gx', 'gy', 'gz')), may hold values from -0.75 to 0.75
- leaf_transfer: float32 [1024, 64, 64], P(('gx', 'gy', 'gz'))
- node_transfer: float32 [32, 5, 64, 64], P(('gx', 'gy', 'gz')), as said below
- node_points: float32 [32, 5, 3, 64], P(('gx', 'gy', 'gz')), as said below
- near_list: int32 [1024, 8], P(('gx', 'gy', 'gz')), may hold values from 0 to 47, as said below
- near_count: int32 [1024], P(('gx', 'gy', 'gz')), may hold values from 1 to 8, as said below
- far_list: int32 [1024, 8], P(('gx', 'gy', 'gz')), may hold values from 0 to 47, as said below
Outputs:
- potential: float32 [1024, 128], P(('gx', 'gy', 'gz'))
The draws below stay inside these ranges and needn't reach their ends.
Inputs may be any that keep to these rules, and one draw needn't show every extreme that they name: `near_list`: entry 0 of the list of a leaf with number i within its device is i + 8; the other entries are distinct positions within 8 of i + 8. `far_list`: distinct positions within 8 of the leaf's own position i + 8, none of them in the leaf's near list. Only the first near_count[g] entries of leaf g's near list are used. `node_transfer`: rows of devices in the same node (k, c) are equal at level k. `node_points`: rows of devices in the same node (k, c) are equal at level k.
All inputs are finite; a program needn't handle non-finite values.
Results may differ from the reference program's by a relative error of at most 0.0003.
Values sent between devices are 32-bit elements; how exact they have to be, the bound alone decides.
A program may use at most 64 MiB of HBM per device.

```python
import jax
import jax.numpy as jnp
from jax import lax

RANK = 64
PTS = 128
NEAR = 8
FAR = 8
LEAF_DEV = 32
HALO = 8
CLUSTERS = 32
LEAVES = 1024
LEVELS = 5


def morton_cell(index, bit_count):
    coords = [jnp.zeros_like(index), jnp.zeros_like(index), jnp.zeros_like(index)]
    for bit_place in range(bit_count):
        coords[bit_place % 3] = coords[bit_place % 3] + ((index >> bit_place & 1) << bit_place // 3)
    return jnp.stack(coords).astype(jnp.float32)


def draw_points(key, part):
    index = jnp.arange(LEAVES, dtype=jnp.int32)
    cells = morton_cell(index, LEAVES.bit_length() - 1)
    unit = jax.random.uniform(key, (LEAVES, 3, PTS), jnp.float32)
    return cells.T[:, :, None] + 2.0 * unit - 0.5


def node_copies(base):
    device = jnp.arange(CLUSTERS, dtype=jnp.int32)
    layers = []
    for level_index in range(LEVELS):
        first = device >> level_index << level_index
        layers.append(base[level_index][first])
    return jnp.stack(layers, axis=1)


def draw_node_points(key, part):
    total_bits = LEAVES.bit_length() - 1
    leaf_bits = LEAF_DEV.bit_length() - 1
    unit = jax.random.uniform(key, (LEVELS, CLUSTERS, 3, RANK), jnp.float32)
    device = jnp.arange(CLUSTERS, dtype=jnp.int32)
    layers = []
    for level_index in range(LEVELS):
        first = device >> level_index << level_index
        corner = morton_cell(first * LEAF_DEV, total_bits)
        span_bits = level_index + leaf_bits
        extent_list = []
        for axis_pick in range(3):
            bit_total = 0
            for bit_place in range(span_bits):
                if bit_place % 3 == axis_pick:
                    bit_total = bit_total + 1
            side_length = 2 ** bit_total
            extent_list.append(float(side_length))
        extent = jnp.array(extent_list, jnp.float32)
        layers.append(corner.T[:, :, None] + extent[None, :, None] * unit[level_index][first])
    return jnp.stack(layers, axis=1)


def draw_node_transfer(key, part):
    scale = 2.0 ** (-0.25) / RANK ** 0.5
    base = jax.random.normal(key, (LEVELS, CLUSTERS, RANK, RANK), jnp.float32) * scale
    return node_copies(base)


def draw_leaf_transfer(key, part):
    scale = LEAF_DEV ** (-0.25) / RANK ** 0.5
    return jax.random.normal(key, (LEAVES, RANK, RANK), jnp.float32) * scale


def neighbor_table(key):
    subkey = jax.random.fold_in(key, 11)
    spread = 2 * HALO
    scores = jax.random.randint(subkey, (LEAVES, spread), 0, 1 << 20) * spread + jnp.arange(spread, dtype=jnp.int32)[None, :]
    order = jnp.argsort(scores, axis=1, stable=True).astype(jnp.int32)
    offset = jnp.where(order < HALO, order - HALO, order - HALO + 1)
    home = jnp.arange(LEAVES, dtype=jnp.int32) % LEAF_DEV + HALO
    window = home[:, None] + offset
    near_part = jnp.concatenate([home[:, None], window[:, :NEAR - 1]], axis=1)
    far_part = window[:, NEAR - 1:NEAR - 1 + FAR]
    return (near_part, far_part)


def draw_near_list(key, part):
    return neighbor_table(key)[0]


def draw_far_list(key, part):
    return neighbor_table(key)[1]


def draw_near_count(key, part):
    first_key = jax.random.fold_in(key, 3)
    second_key = jax.random.fold_in(key, 5)
    third_key = jax.random.fold_in(key, 9)
    device_level = jax.random.randint(first_key, (CLUSTERS,), 1, NEAR + 1)
    per_leaf = jax.random.randint(second_key, (CLUSTERS, LEAF_DEV), 0, 1 << 20) % device_level[:, None] + 1
    chosen = jax.random.randint(third_key, (), 0, LEAVES)
    counts = per_leaf.reshape(LEAVES)
    return jnp.where(jnp.arange(LEAVES, dtype=jnp.int32) == chosen, NEAR, counts).astype(jnp.int32)


def block_scale(rng, shape, shards, smallest, largest):
    def one(axis_at, shards_of):
        draws = jax.random.uniform(jax.random.fold_in(jax.random.fold_in(rng, 6), axis_at), (shards_of,), jnp.float32, smallest / len(shards), largest / len(shards))
        return jnp.repeat(jnp.exp(draws), shape[axis_at] // shards_of).reshape((-1,) + (1,) * (len(shape) - axis_at - 1))

    factor_of = one(*shards[0])
    for cut in shards[1:]:
        factor_of = factor_of * one(*cut)
    return factor_of


def centred(stream_key, shape, scale, reach, cuts=(), kind=jnp.bfloat16):
    values = scale * jax.random.normal(stream_key, shape, jnp.float32)
    if cuts:
        values = values * block_scale(stream_key, shape, cuts, -0.22, 0.18)
    return jnp.clip(values, -reach, reach).astype(kind)


def setup_inputs(seed: int = 0) -> dict:
    key_of = jax.random.split(jax.random.key(seed), 10)
    return {
        "points": draw_points(jax.random.fold_in(key_of[9], 71), 0),
        "charges": centred(key_of[1], (LEAVES, PTS), 0.1, 0.6, ((0, 32),), jnp.float32),
        "interpolant": centred(key_of[2], (LEAVES, RANK, PTS - RANK), (PTS - RANK) ** -0.5, 0.75, ((0, 32),), jnp.float32),
        "leaf_transfer": draw_leaf_transfer(jax.random.fold_in(key_of[9], 71), 0),
        "node_transfer": draw_node_transfer(jax.random.fold_in(key_of[9], 71), 0),
        "node_points": draw_node_points(jax.random.fold_in(key_of[9], 71), 0),
        "near_list": draw_near_list(jax.random.fold_in(key_of[9], 71), 0),
        "near_count": draw_near_count(jax.random.fold_in(key_of[9], 71), 0),
        "far_list": draw_far_list(jax.random.fold_in(key_of[9], 71), 0),
    }


SOFTENING = 0.0625
HIGHEST = lax.Precision.HIGHEST

def kernel(targets, sources):
    spread = targets[..., :, :, None] - sources[..., :, None, :]
    return lax.rsqrt(lax.optimization_barrier(jnp.sum(spread * spread, axis=-3)) + SOFTENING)

def leaf_terms(window, near_list, near_count, far_list, skeleton_rank):
    leaves = near_list.shape[0]
    margin = (window.shape[0] - leaves) // 2
    targets = window[margin:margin + leaves]
    blocks = leaves // 4

    def block_terms(pieces):
        target_block, near_block, count_block, far_block = pieces
        sources = window[near_block]
        slot_index = jnp.arange(near_block.shape[1], dtype=jnp.int32)
        is_live = slot_index[None, :] < count_block[:, None]
        weights = jnp.where(is_live[:, :, None], sources[:, :, 3, :], 0.0)
        kernel_tiles = kernel(target_block[:, None, 0:3, :], sources[:, :, 0:3, :])
        near_part = jnp.einsum('bmpq,bmq->bp', kernel_tiles, weights, precision=HIGHEST)
        distant = window[far_block]
        coupling = kernel(target_block[:, None, 0:3, :skeleton_rank], distant[:, :, 0:3, :skeleton_rank])
        far_part = jnp.einsum('bmpq,bmq->bp', coupling, distant[:, :, 4, :skeleton_rank], precision=HIGHEST)
        return (near_part, far_part)
    near_part, far_part = lax.map(block_terms, (targets.reshape((blocks, 4) + targets.shape[1:]), near_list.reshape(blocks, 4, near_list.shape[1]), near_count.reshape(blocks, 4), far_list.reshape(blocks, 4, far_list.shape[1])))
    return (near_part.reshape(leaves, near_part.shape[2]), far_part.reshape(leaves, far_part.shape[2]))

def reference(points, charges, interpolant, leaf_transfer, node_transfer, node_points, near_list, near_count, far_list):
    skeleton = charges[:, :RANK] + jnp.einsum('lrp,lp->lr', interpolant, charges[:, RANK:], precision=HIGHEST)
    packed = jnp.concatenate([points, charges[:, None, :], jnp.pad(skeleton, ((0, 0), (0, PTS - RANK)))[:, None, :]], axis=1)
    padded = jnp.pad(packed, ((HALO, HALO), (0, 0), (0, 0)))
    blocks_up = leaf_transfer.reshape(CLUSTERS, LEAF_DEV, RANK, RANK)
    device_skeleton = jnp.einsum('dirc,dir->dc', blocks_up, skeleton.reshape(CLUSTERS, LEAF_DEV, RANK), precision=HIGHEST)
    current = device_skeleton
    couplings = []
    for level_index in range(LEVELS):
        stride = 2 ** level_index
        transfer_rows = node_transfer[::stride, level_index]
        centres = node_points[::stride, level_index]
        count_nodes = current.shape[0]
        swapped = current.reshape(count_nodes // 2, 2, RANK)[:, ::-1].reshape(count_nodes, RANK)
        partner_centres = centres.reshape(count_nodes // 2, 2, 3, RANK)[:, ::-1].reshape(count_nodes, 3, RANK)
        couplings.append(jnp.einsum('nab,nb->na', kernel(centres, partner_centres), swapped, precision=HIGHEST))
        lifted = jnp.einsum('nrc,nr->nc', transfer_rows, current, precision=HIGHEST)
        current = lifted.reshape(count_nodes // 2, 2, RANK).sum(axis=1)
    expansion = couplings[-1]
    for level_index in range(LEVELS - 1, 0, -1):
        stride = 2 ** (level_index - 1)
        transfer_rows = node_transfer[::stride, level_index - 1]
        parents = jnp.repeat(expansion, 2, axis=0)
        expansion = couplings[level_index - 1] + jnp.einsum('nrc,nc->nr', transfer_rows, parents, precision=HIGHEST)
    from_device = jnp.einsum('dirc,dc->dir', blocks_up, expansion, precision=HIGHEST).reshape(LEAVES, RANK)

    def device_terms(device):
        start = (device * LEAF_DEV).astype(jnp.int32)
        window = lax.dynamic_slice_in_dim(padded, start, LEAF_DEV + 2 * HALO, 0)
        near_rows = lax.dynamic_slice_in_dim(near_list, start, LEAF_DEV, 0)
        count_rows = lax.dynamic_slice_in_dim(near_count, start, LEAF_DEV, 0)
        far_rows = lax.dynamic_slice_in_dim(far_list, start, LEAF_DEV, 0)
        return leaf_terms(window, near_rows, count_rows, far_rows, RANK)
    near_part, far_part = lax.map(device_terms, jnp.arange(CLUSTERS, dtype=jnp.int32))
    combined = far_part.reshape(LEAVES, RANK) + from_device
    upper = jnp.einsum('lrp,lr->lp', interpolant, combined, precision=HIGHEST)
    return jnp.concatenate([combined, upper], axis=1) + near_part.reshape(LEAVES, PTS)
```

```python
import functools
import math

import jax
import jax.numpy as jnp
from jax import lax
from jax.experimental import pallas as pl
from jax.experimental.pallas import tpu as pltpu
from jax.sharding import PartitionSpec as P

HALO = 8
SOFTENING = 0.0625
MESH = pl.DeviceIdType.MESH
AXES = ("gx", "gy", "gz")
CHUNK = 32


def flipped(place, mask):
    result = place
    bit = 1
    while bit <= mask:
        if mask & bit:
            result = result + bit - 2 * bit * ((place // bit) % 2)
        bit *= 2
    return result


def total_lanes(value):
    return jnp.sum(value, axis=1, keepdims=True)


def total_rows(value):
    return jnp.sum(value, axis=0, keepdims=True)


def softened(tx, ty, tz, sx, sy, sz):
    dx = tx - sx
    dy = ty - sy
    dz = tz - sz
    return lax.rsqrt(dx * dx + dy * dy + dz * dz + SOFTENING)


def body(
    sizes,
    near_ref,
    count_ref,
    far_ref,
    points_ref,
    charges_ref,
    interp_hbm,
    transfer_hbm,
    node_transfer_ref,
    node_points_ref,
    out_ref,
    interp_ref,
    transfer_ref,
    turned_ref,
    own_ref,
    win_ref,
    column_ref,
    far_acc_ref,
    coupling_ref,
    node_col_ref,
    pay_ref,
    recv_ref,
    load_sem,
    halo_send,
    halo_recv,
    tree_send,
    tree_recv,
):
    leaves, _, pts = points_ref.shape
    rank = interp_ref.shape[1]
    near_slots = near_ref.shape[1]
    far_slots = far_ref.shape[1]
    levels = node_transfer_ref.shape[1]
    gx, gy, gz = (lax.axis_index(name) for name in AXES)
    nx, ny, nz = sizes
    count = nx * ny * nz
    me = (gx * ny + gy) * nz + gz
    where_of = {"gx": gx, "gy": gy, "gz": gz}
    size_of = dict(zip(AXES, sizes))
    phases = [name for name in ("gz", "gy", "gx") if size_of[name] > 1]

    def address(index):
        return {
            "gx": index // (ny * nz),
            "gy": (index // nz) % ny,
            "gz": index % nz,
        }

    left = address((me + count - 1) % count)
    right = address((me + 1) % count)

    interp_copy = pltpu.make_async_copy(interp_hbm, interp_ref, load_sem.at[0])
    transfer_copy = pltpu.make_async_copy(transfer_hbm, transfer_ref, load_sem.at[1])
    interp_copy.start()
    transfer_copy.start()

    barrier = pltpu.get_barrier_semaphore()
    greeted = 2
    pl.semaphore_signal(barrier, inc=1, device_id=left, device_id_type=MESH)
    pl.semaphore_signal(barrier, inc=1, device_id=right, device_id_type=MESH)
    for name in phases:
        for mask in range(1, size_of[name]):
            pl.semaphore_signal(
                barrier,
                inc=1,
                device_id={name: flipped(where_of[name], mask)},
                device_id_type=MESH,
            )
            greeted += 1

    def unit(n):
        return (
            lax.broadcasted_iota(jnp.int32, (n, n), 0)
            == lax.broadcasted_iota(jnp.int32, (n, n), 1)
        ).astype(jnp.float32)

    eye = unit(rank)
    eye_pts = unit(pts)

    turned_ref[...] = jnp.concatenate(
        [charges_ref[:, rank:], charges_ref[:, :rank]], axis=1
    )
    own_ref[...] = jnp.zeros_like(own_ref)
    pay_ref[...] = jnp.zeros_like(pay_ref)
    own_ref[HALO : HALO + leaves, 0:3, :] = points_ref[...]

    for level in range(levels):
        for dim in range(3):
            node_col_ref[3 * level + dim] = jnp.broadcast_to(
                total_lanes(eye * node_points_ref[0, level, dim : dim + 1, :]), (rank, rank)
            )

    interp_copy.wait()
    transfer_copy.wait()

    def skeleton_step(step, acc):
        for part in range(4):
            leaf = step * 4 + part
            upper = turned_ref[pl.ds(leaf, 1), :]
            row = charges_ref[pl.ds(leaf, 1), :]
            col = total_lanes(interp_ref[leaf] * upper[:, :rank] + eye * row[:, :rank])
            own_ref[HALO + leaf, 3:4, :] = row
            own_ref[HALO + leaf, 4:5, 0:rank] = total_rows(eye * col)
            acc = acc + transfer_ref[leaf] * col
        return acc

    acc = lax.fori_loop(0, leaves // 4, skeleton_step, jnp.zeros((rank, rank), jnp.float32))
    node_row = total_rows(acc)

    pl.semaphore_wait(barrier, greeted)
    halo_copies = [
        pltpu.make_async_remote_copy(
            src_ref=own_ref.at[pl.ds(HALO, HALO)],
            dst_ref=win_ref.at[pl.ds(leaves + HALO, HALO)],
            send_sem=halo_send.at[0],
            recv_sem=halo_recv.at[0],
            device_id=left,
            device_id_type=MESH,
        ),
        pltpu.make_async_remote_copy(
            src_ref=own_ref.at[pl.ds(leaves, HALO)],
            dst_ref=win_ref.at[pl.ds(0, HALO)],
            send_sem=halo_send.at[1],
            recv_sem=halo_recv.at[1],
            device_id=right,
            device_id_type=MESH,
        ),
    ]
    for copy in halo_copies:
        copy.start()
    win_ref[HALO : HALO + leaves] = own_ref[HALO : HALO + leaves]

    def set_targets(leaf):
        tile = jnp.transpose(own_ref[HALO + leaf])
        for dim in range(3):
            column_ref[dim] = jnp.broadcast_to(tile[:, dim : dim + 1], (pts, pts))

    low_half = lax.broadcasted_iota(jnp.int32, (8, pts), 1) < rank

    def leaf_step(source_ref, leaf):
        set_targets(leaf)
        live = count_ref[leaf]
        places = [near_ref[leaf, m] for m in range(near_slots)]
        weights = [
            jnp.where(m < live, source_ref[places[m], 3:4, :], 0.0) for m in range(near_slots)
        ]
        near_cols = []
        for start in range(0, pts, CHUNK):
            tx, ty, tz = (column_ref[dim, start : start + CHUNK, :] for dim in range(3))
            total = jnp.zeros((CHUNK, pts), jnp.float32)
            for m in range(near_slots):
                sx, sy, sz = (source_ref[places[m], dim : dim + 1, :] for dim in range(3))
                total = total + softened(tx, ty, tz, sx, sy, sz) * weights[m]
            near_cols.append(total_lanes(total))
        near_col = jnp.concatenate(near_cols, axis=0)
        out_ref[pl.ds(leaf, 1), :] = total_rows(eye_pts * near_col)
        pairs = []
        for m in range(0, far_slots, 2):
            first = source_ref[far_ref[leaf, m]]
            second = source_ref[far_ref[leaf, m + 1]]
            pairs.append(jnp.where(low_half, first, pltpu.roll(second, rank, 1)))
        for start in range(0, rank, CHUNK):
            tx, ty, tz = (column_ref[dim, start : start + CHUNK, :] for dim in range(3))
            total = jnp.zeros((CHUNK, pts), jnp.float32)
            for pair in pairs:
                total = total + softened(
                    tx, ty, tz, pair[0:1], pair[1:2], pair[2:3]
                ) * pair[4:5]
            far_acc_ref[leaf, start : start + CHUNK, :] = total

    def run_leaves(source_ref, first, last):
        def step(leaf, carry):
            leaf_step(source_ref, leaf)
            return carry

        lax.fori_loop(first, last, step, 0)

    inner = leaves - 2 * HALO
    level = 0
    pay_at = 0
    recv_at = 0
    for order, name in enumerate(phases):
        bits = size_of[name].bit_length() - 1
        last_phase = order == len(phases) - 1
        chain = [node_row]
        for step in range(bits):
            if last_phase and step == bits - 1:
                chain.append(chain[-1])
            else:
                col = total_lanes(eye * chain[-1])
                chain.append(total_rows(node_transfer_ref[0, level + step] * col))
        for step in range(bits):
            pay_ref[pay_at + step, 0:1, 0:rank] = chain[step]
            pay_ref[pay_at + step, 1:4, 0:rank] = node_points_ref[0, level + step]
            pay_ref[pay_at + step, 4:5, 0:rank] = chain[bits]
        copies = []
        for mask in range(1, size_of[name]):
            step = mask.bit_length() - 1
            slot = recv_at + mask - 1
            copy = pltpu.make_async_remote_copy(
                src_ref=pay_ref.at[pay_at + step],
                dst_ref=recv_ref.at[slot],
                send_sem=tree_send.at[slot],
                recv_sem=tree_recv.at[slot],
                device_id={name: flipped(where_of[name], mask)},
                device_id_type=MESH,
            )
            copy.start()
            copies.append(copy)
        first = HALO + inner * order // len(phases)
        last = HALO + inner * (order + 1) // len(phases)
        run_leaves(own_ref, first, last)
        if last_phase:
            for copy in halo_copies:
                copy.wait()

            @pl.when(me == 0)
            def _():
                win_ref[0:HALO] = jnp.zeros((HALO, 8, pts), jnp.float32)

            @pl.when(me == count - 1)
            def _():
                win_ref[leaves + HALO :] = jnp.zeros((HALO, 8, pts), jnp.float32)

            run_leaves(win_ref, 0, HALO)
            run_leaves(win_ref, leaves - HALO, leaves)
        for copy in copies:
            copy.wait()
        node_row = chain[bits]
        for mask in range(1, size_of[name]):
            node_row = node_row + recv_ref[recv_at + mask - 1, 4:5, 0:rank]
        for step in range(bits):
            base = recv_at + 2**step - 1
            sibling = recv_ref[base, 0:1, 0:rank]
            for other in range(1, 2**step):
                sibling = sibling + recv_ref[base + other, 0:1, 0:rank]
            targets = [node_col_ref[3 * (level + step) + dim] for dim in range(3)]
            sources = [recv_ref[base, 1 + dim : 2 + dim, 0:rank] for dim in range(3)]
            coupling_ref[level + step] = softened(*targets, *sources) * sibling
        level += bits
        pay_at += bits
        recv_at += size_of[name] - 1

    expansion = total_lanes(coupling_ref[levels - 1])
    for level in range(levels - 2, -1, -1):
        expansion = total_lanes(
            coupling_ref[level] + node_transfer_ref[0, level] * total_rows(eye * expansion)
        )
    expansion_row = total_rows(eye * expansion)

    def finish_step(step, carry):
        for part in range(4):
            leaf = step * 4 + part
            combined = total_lanes(transfer_ref[leaf] * expansion_row) + total_lanes(
                far_acc_ref[leaf]
            )
            row = jnp.concatenate(
                [total_rows(eye * combined), total_rows(interp_ref[leaf] * combined)], axis=1
            )
            out_ref[pl.ds(leaf, 1), :] = out_ref[pl.ds(leaf, 1), :] + row
        return carry

    lax.fori_loop(0, leaves // 4, finish_step, 0)


def on_device(
    sizes,
    points,
    charges,
    interpolant,
    leaf_transfer,
    node_transfer,
    node_points,
    near_list,
    near_count,
    far_list,
):
    leaves, _, pts = points.shape
    rank = interpolant.shape[1]
    levels = node_transfer.shape[1]
    peers = sum(size - 1 for size in sizes)
    smem = pl.BlockSpec(memory_space=pltpu.SMEM)
    vmem = pl.BlockSpec(memory_space=pltpu.VMEM)
    hbm = pl.BlockSpec(memory_space=pl.ANY)
    f32 = jnp.float32
    return pl.pallas_call(
        functools.partial(body, sizes),
        out_shape=jax.ShapeDtypeStruct(charges.shape, f32),
        in_specs=[smem, smem, smem, vmem, vmem, hbm, hbm, vmem, vmem],
        out_specs=vmem,
        scratch_shapes=[
            pltpu.VMEM(interpolant.shape, f32),
            pltpu.VMEM(leaf_transfer.shape, f32),
            pltpu.VMEM(charges.shape, f32),
            pltpu.VMEM((leaves + 2 * HALO, 8, pts), f32),
            pltpu.VMEM((leaves + 2 * HALO, 8, pts), f32),
            pltpu.VMEM((3, pts, pts), f32),
            pltpu.VMEM((leaves, rank, pts), f32),
            pltpu.VMEM((levels, rank, rank), f32),
            pltpu.VMEM((3 * levels, rank, rank), f32),
            pltpu.VMEM((levels, 8, pts), f32),
            pltpu.VMEM((peers, 8, pts), f32),
            pltpu.SemaphoreType.DMA((2,)),
            pltpu.SemaphoreType.DMA((2,)),
            pltpu.SemaphoreType.DMA((2,)),
            pltpu.SemaphoreType.DMA((peers,)),
            pltpu.SemaphoreType.DMA((peers,)),
        ],
        compiler_params=pltpu.CompilerParams(
            collective_id=0, has_side_effects=True, vmem_limit_bytes=40 * 2**20
        ),
    )(
        near_list,
        near_count,
        far_list,
        points,
        charges,
        interpolant,
        leaf_transfer,
        node_transfer,
        node_points,
    )


def solution(mesh):
    sizes = tuple(mesh.shape[name] for name in AXES)
    return jax.shard_map(
        functools.partial(on_device, sizes),
        mesh=mesh,
        in_specs=(
            P(AXES, None, None),
            P(AXES, None),
            P(AXES, None, None),
            P(AXES, None, None),
            P(AXES, None, None, None),
            P(AXES, None, None, None),
            P(AXES, None),
            P(AXES),
            P(AXES, None),
        ),
        out_specs=P(AXES, None),
        check_vma=False,
    )
```

```python
import functools

import jax
import jax.numpy as jnp
from jax import lax
from jax.experimental import pallas as pl
from jax.experimental.pallas import tpu as pltpu
from jax.sharding import PartitionSpec as P

HALO = 8
SOFTENING = 0.0625
MESH = pl.DeviceIdType.MESH
AXES = ("gx", "gy", "gz")
CHUNK = 32


def flipped(place, mask):
    result = place
    bit = 1
    while bit <= mask:
        if mask & bit:
            result = result + bit - 2 * bit * ((place // bit) % 2)
        bit *= 2
    return result


def total_lanes(value):
    return jnp.sum(value, axis=1, keepdims=True)


def total_rows(value):
    return jnp.sum(value, axis=0, keepdims=True)


def softened(tx, ty, tz, sx, sy, sz):
    dx = tx - sx
    dy = ty - sy
    dz = tz - sz
    return lax.rsqrt(dx * dx + dy * dy + dz * dz + SOFTENING)


def body(
    sizes,
    near_hbm,
    count_hbm,
    far_hbm,
    points_hbm,
    charges_hbm,
    interp_hbm,
    transfer_hbm,
    node_transfer_hbm,
    node_points_hbm,
    out_ref,
    near_ref,
    count_ref,
    far_ref,
    points_ref,
    charges_ref,
    interp_ref,
    transfer_ref,
    node_transfer_ref,
    node_points_ref,
    turned_ref,
    own_ref,
    win_ref,
    column_ref,
    far_acc_ref,
    coupling_ref,
    node_col_ref,
    pay_ref,
    recv_ref,
    load_sem,
    halo_send,
    halo_recv,
    tree_send,
    tree_recv,
):
    leaves, pts = charges_ref.shape
    rank = interp_ref.shape[1]
    near_slots = near_ref.shape[0]
    far_slots = far_ref.shape[0]
    levels = node_transfer_ref.shape[1]
    gx, gy, gz = (lax.axis_index(name) for name in AXES)
    nx, ny, nz = sizes
    count = nx * ny * nz
    me = (gx * ny + gy) * nz + gz
    where_of = {"gx": gx, "gy": gy, "gz": gz}
    size_of = dict(zip(AXES, sizes))
    phases = [name for name in ("gz", "gy", "gx") if size_of[name] > 1]

    def address(index):
        return {
            "gx": index // (ny * nz),
            "gy": (index // nz) % ny,
            "gz": index % nz,
        }

    left = address((me + count - 1) % count)
    right = address((me + 1) % count)

    loads = [
        pltpu.make_async_copy(source, target, load_sem.at[at])
        for at, (source, target) in enumerate(
            (
                (points_hbm, points_ref),
                (charges_hbm, charges_ref),
                (interp_hbm, interp_ref),
                (transfer_hbm, transfer_ref),
                (node_points_hbm, node_points_ref),
                (node_transfer_hbm, node_transfer_ref),
                (near_hbm, near_ref),
                (count_hbm, count_ref),
                (far_hbm, far_ref),
            )
        )
    ]
    for load in loads:
        load.start()

    barrier = pltpu.get_barrier_semaphore()
    greeted = 2
    pl.semaphore_signal(barrier, inc=1, device_id=left, device_id_type=MESH)
    pl.semaphore_signal(barrier, inc=1, device_id=right, device_id_type=MESH)
    for name in phases:
        for mask in range(1, size_of[name]):
            pl.semaphore_signal(
                barrier,
                inc=1,
                device_id={name: flipped(where_of[name], mask)},
                device_id_type=MESH,
            )
            greeted += 1

    def unit(n):
        return (
            lax.broadcasted_iota(jnp.int32, (n, n), 0)
            == lax.broadcasted_iota(jnp.int32, (n, n), 1)
        ).astype(jnp.float32)

    eye = unit(rank)
    eye_pts = unit(pts)

    own_ref[...] = jnp.zeros_like(own_ref)
    pay_ref[...] = jnp.zeros_like(pay_ref)
    loads[0].wait()
    loads[1].wait()
    turned_ref[...] = jnp.concatenate(
        [charges_ref[:, rank:], charges_ref[:, :rank]], axis=1
    )

    def target_step(step, carry):
        for part in range(4):
            leaf = step * 4 + part
            rows = [points_ref[dim, pl.ds(leaf, 1), :] for dim in range(3)]
            for dim in range(3):
                own_ref[HALO + leaf, dim : dim + 1, :] = rows[dim]
            own_ref[HALO + leaf, 3:4, :] = charges_ref[pl.ds(leaf, 1), :]
            tile = jnp.transpose(jnp.concatenate(rows + [jnp.zeros((5, pts), jnp.float32)], axis=0))
            for dim in range(3):
                column_ref[leaf, dim] = jnp.broadcast_to(tile[:, dim : dim + 1], (pts, pts))
        return carry

    lax.fori_loop(0, leaves // 4, target_step, 0)

    loads[4].wait()
    for level in range(levels):
        for dim in range(3):
            node_col_ref[3 * level + dim] = jnp.broadcast_to(
                total_lanes(eye * node_points_ref[level, dim]), (rank, rank)
            )

    for load in loads[2:4] + loads[5:]:
        load.wait()

    def skeleton_step(step, acc):
        for part in range(4):
            leaf = step * 4 + part
            upper = turned_ref[pl.ds(leaf, 1), :]
            row = charges_ref[pl.ds(leaf, 1), :]
            col = total_lanes(interp_ref[leaf] * upper[:, :rank] + eye * row[:, :rank])
            own_ref[HALO + leaf, 4:5, 0:rank] = total_rows(eye * col)
            acc = acc + transfer_ref[leaf] * col
        return acc

    acc = lax.fori_loop(0, leaves // 4, skeleton_step, jnp.zeros((rank, rank), jnp.float32))
    node_row = total_rows(acc)

    pl.semaphore_wait(barrier, greeted)
    halo_copies = [
        pltpu.make_async_remote_copy(
            src_ref=own_ref.at[pl.ds(HALO, HALO)],
            dst_ref=win_ref.at[pl.ds(leaves + HALO, HALO)],
            send_sem=halo_send.at[0],
            recv_sem=halo_recv.at[0],
            device_id=left,
            device_id_type=MESH,
        ),
        pltpu.make_async_remote_copy(
            src_ref=own_ref.at[pl.ds(leaves, HALO)],
            dst_ref=win_ref.at[pl.ds(0, HALO)],
            send_sem=halo_send.at[1],
            recv_sem=halo_recv.at[1],
            device_id=right,
            device_id_type=MESH,
        ),
    ]
    for copy in halo_copies:
        copy.start()
    win_ref[HALO : HALO + leaves] = own_ref[HALO : HALO + leaves]

    low_half = lax.broadcasted_iota(jnp.int32, (8, pts), 1) < rank

    def leaf_step(source_ref, leaf):
        live = count_ref[leaf]
        places = [near_ref[m, leaf] for m in range(near_slots)]
        weights = [
            jnp.where(m < live, source_ref[places[m], 3:4, :], 0.0) for m in range(near_slots)
        ]
        near_cols = []
        for start in range(0, pts, CHUNK):
            tx, ty, tz = (column_ref[leaf, dim, start : start + CHUNK, :] for dim in range(3))
            total = jnp.zeros((CHUNK, pts), jnp.float32)
            for m in range(near_slots):
                sx, sy, sz = (source_ref[places[m], dim : dim + 1, :] for dim in range(3))
                total = total + softened(tx, ty, tz, sx, sy, sz) * weights[m]
            near_cols.append(total_lanes(total))
        near_col = jnp.concatenate(near_cols, axis=0)
        out_ref[pl.ds(leaf, 1), :] = total_rows(eye_pts * near_col)
        pairs = []
        for m in range(0, far_slots, 2):
            first = source_ref[far_ref[m, leaf]]
            second = source_ref[far_ref[m + 1, leaf]]
            pairs.append(jnp.where(low_half, first, pltpu.roll(second, rank, 1)))
        for start in range(0, rank, CHUNK):
            tx, ty, tz = (column_ref[leaf, dim, start : start + CHUNK, :] for dim in range(3))
            total = jnp.zeros((CHUNK, pts), jnp.float32)
            for pair in pairs:
                total = total + softened(
                    tx, ty, tz, pair[0:1], pair[1:2], pair[2:3]
                ) * pair[4:5]
            far_acc_ref[leaf, start : start + CHUNK, :] = total

    def run_leaves(source_ref, first, last):
        def step(pair, carry):
            leaf_step(source_ref, first + 2 * pair)
            leaf_step(source_ref, first + 2 * pair + 1)
            return carry

        lax.fori_loop(0, (last - first) // 2, step, 0)

    inner = leaves - 2 * HALO
    level = 0
    pay_at = 0
    recv_at = 0
    for order, name in enumerate(phases):
        bits = size_of[name].bit_length() - 1
        last_phase = order == len(phases) - 1
        chain = [node_row]
        for step in range(bits):
            if last_phase and step == bits - 1:
                chain.append(chain[-1])
            else:
                col = total_lanes(eye * chain[-1])
                chain.append(total_rows(node_transfer_ref[0, level + step] * col))
        for step in range(bits):
            pay_ref[pay_at + step, 0:1, 0:rank] = chain[step]
            for dim in range(3):
                pay_ref[pay_at + step, 1 + dim : 2 + dim, 0:rank] = node_points_ref[
                    level + step, dim
                ]
            pay_ref[pay_at + step, 4:5, 0:rank] = chain[bits]
        copies = []
        for mask in range(1, size_of[name]):
            step = mask.bit_length() - 1
            slot = recv_at + mask - 1
            copy = pltpu.make_async_remote_copy(
                src_ref=pay_ref.at[pay_at + step],
                dst_ref=recv_ref.at[slot],
                send_sem=tree_send.at[slot],
                recv_sem=tree_recv.at[slot],
                device_id={name: flipped(where_of[name], mask)},
                device_id_type=MESH,
            )
            copy.start()
            copies.append(copy)
        if not last_phase:
            spans = max(len(phases) - 1, 1)
            first = HALO + inner * order // spans // 2 * 2
            last = HALO + inner * (order + 1) // spans // 2 * 2
            run_leaves(own_ref, first, last)
        if last_phase:
            for copy in halo_copies:
                copy.wait()

            @pl.when(me == 0)
            def _():
                win_ref[0:HALO] = jnp.zeros((HALO, 8, pts), jnp.float32)

            @pl.when(me == count - 1)
            def _():
                win_ref[leaves + HALO :] = jnp.zeros((HALO, 8, pts), jnp.float32)

            run_leaves(win_ref, 0, HALO)
            run_leaves(win_ref, leaves - HALO, leaves)
        for copy in copies:
            copy.wait()
        node_row = chain[bits]
        for mask in range(1, size_of[name]):
            node_row = node_row + recv_ref[recv_at + mask - 1, 4:5, 0:rank]
        for step in range(bits):
            base = recv_at + 2**step - 1
            sibling = recv_ref[base, 0:1, 0:rank]
            for other in range(1, 2**step):
                sibling = sibling + recv_ref[base + other, 0:1, 0:rank]
            targets = [node_col_ref[3 * (level + step) + dim] for dim in range(3)]
            sources = [recv_ref[base, 1 + dim : 2 + dim, 0:rank] for dim in range(3)]
            coupling_ref[level + step] = softened(*targets, *sources) * sibling
        level += bits
        pay_at += bits
        recv_at += size_of[name] - 1

    expansion = total_lanes(coupling_ref[levels - 1])
    for level in range(levels - 2, -1, -1):
        expansion = total_lanes(
            coupling_ref[level] + node_transfer_ref[0, level] * total_rows(eye * expansion)
        )
    expansion_row = total_rows(eye * expansion)

    def finish_step(step, carry):
        for part in range(4):
            leaf = step * 4 + part
            combined = total_lanes(transfer_ref[leaf] * expansion_row) + total_lanes(
                far_acc_ref[leaf]
            )
            row = jnp.concatenate(
                [total_rows(eye * combined), total_rows(interp_ref[leaf] * combined)], axis=1
            )
            out_ref[pl.ds(leaf, 1), :] = out_ref[pl.ds(leaf, 1), :] + row
        return carry

    lax.fori_loop(0, leaves // 4, finish_step, 0)


def on_device(
    sizes,
    points,
    charges,
    interpolant,
    leaf_transfer,
    node_transfer,
    node_points,
    near_list,
    near_count,
    far_list,
):
    points = points.transpose(1, 0, 2)
    node_points = node_points.transpose(1, 2, 0, 3)
    near_list = near_list.T
    far_list = far_list.T
    leaves, pts = charges.shape
    rank = interpolant.shape[1]
    levels = node_transfer.shape[1]
    peers = sum(size - 1 for size in sizes)
    vmem = pl.BlockSpec(memory_space=pltpu.VMEM)
    hbm = pl.BlockSpec(memory_space=pl.ANY)
    f32 = jnp.float32
    return pl.pallas_call(
        functools.partial(body, sizes),
        out_shape=jax.ShapeDtypeStruct(charges.shape, f32),
        in_specs=[hbm] * 9,
        out_specs=vmem,
        scratch_shapes=[
            pltpu.SMEM(near_list.shape, jnp.int32),
            pltpu.SMEM(near_count.shape, jnp.int32),
            pltpu.SMEM(far_list.shape, jnp.int32),
            pltpu.VMEM(points.shape, f32),
            pltpu.VMEM(charges.shape, f32),
            pltpu.VMEM(interpolant.shape, f32),
            pltpu.VMEM(leaf_transfer.shape, f32),
            pltpu.VMEM(node_transfer.shape, f32),
            pltpu.VMEM(node_points.shape, f32),
            pltpu.VMEM(charges.shape, f32),
            pltpu.VMEM((leaves + 2 * HALO, 8, pts), f32),
            pltpu.VMEM((leaves + 2 * HALO, 8, pts), f32),
            pltpu.VMEM((leaves, 3, pts, pts), f32),
            pltpu.VMEM((leaves, rank, pts), f32),
            pltpu.VMEM((levels, rank, rank), f32),
            pltpu.VMEM((3 * levels, rank, rank), f32),
            pltpu.VMEM((levels, 8, pts), f32),
            pltpu.VMEM((peers, 8, pts), f32),
            pltpu.SemaphoreType.DMA((9,)),
            pltpu.SemaphoreType.DMA((2,)),
            pltpu.SemaphoreType.DMA((2,)),
            pltpu.SemaphoreType.DMA((peers,)),
            pltpu.SemaphoreType.DMA((peers,)),
        ],
        compiler_params=pltpu.CompilerParams(
            collective_id=0, has_side_effects=True, vmem_limit_bytes=63 * 2**20
        ),
    )(
        near_list,
        near_count,
        far_list,
        points,
        charges,
        interpolant,
        leaf_transfer,
        node_transfer,
        node_points,
    )


def solution(mesh):
    sizes = tuple(mesh.shape[name] for name in AXES)
    return jax.shard_map(
        functools.partial(on_device, sizes),
        mesh=mesh,
        in_specs=(
            P(AXES, None, None),
            P(AXES, None),
            P(AXES, None, None),
            P(AXES, None, None),
            P(AXES, None, None, None),
            P(AXES, None, None, None),
            P(AXES, None),
            P(AXES),
            P(AXES, None),
        ),
        out_specs=P(AXES, None),
        check_vma=False,
    )
```

```python
import functools

import jax
import jax.numpy as jnp
from jax import lax
from jax.experimental import pallas as pl
from jax.experimental.pallas import tpu as pltpu
from jax.sharding import PartitionSpec as P

HALO = 8
SOFTENING = 0.0625
MESH = pl.DeviceIdType.MESH
AXES = ("gx", "gy", "gz")
CHUNK = 32


def flipped(place, mask):
    result = place
    bit = 1
    while bit <= mask:
        if mask & bit:
            result = result + bit - 2 * bit * ((place // bit) % 2)
        bit *= 2
    return result


def total_lanes(value):
    return jnp.sum(value, axis=1, keepdims=True)


def total_rows(value):
    return jnp.sum(value, axis=0, keepdims=True)


def softened(tx, ty, tz, sx, sy, sz):
    dx = tx - sx
    dy = ty - sy
    dz = tz - sz
    return lax.rsqrt(dx * dx + dy * dy + dz * dz + SOFTENING)


def set_columns(column_ref, place, tile):
    turned = jnp.transpose(tile)
    rows = tile.shape[1]
    for dim in range(4):
        column_ref[place, dim] = jnp.broadcast_to(turned[:, dim : dim + 1], (rows, rows))


def body(
    sizes,
    far_hbm,
    points_hbm,
    charges_hbm,
    interp_hbm,
    transfer_hbm,
    node_transfer_hbm,
    node_points_hbm,
    out_ref,
    win_ref,
    far_ref,
    points_ref,
    charges_ref,
    interp_ref,
    transfer_ref,
    node_transfer_ref,
    node_points_ref,
    turned_ref,
    own_ref,
    column_ref,
    far_acc_ref,
    coupling_ref,
    node_col_ref,
    pay_ref,
    recv_ref,
    load_sem,
    halo_send,
    halo_recv,
    tree_send,
    tree_recv,
):
    leaves, pts = charges_ref.shape
    rank = interp_ref.shape[1]
    far_slots = far_ref.shape[0]
    levels = node_transfer_ref.shape[1]
    gx, gy, gz = (lax.axis_index(name) for name in AXES)
    nx, ny, nz = sizes
    count = nx * ny * nz
    me = (gx * ny + gy) * nz + gz
    where_of = {"gx": gx, "gy": gy, "gz": gz}
    size_of = dict(zip(AXES, sizes))
    phases = [name for name in ("gz", "gy", "gx") if size_of[name] > 1]

    def address(index):
        return {
            "gx": index // (ny * nz),
            "gy": (index // nz) % ny,
            "gz": index % nz,
        }

    left = address((me + count - 1) % count)
    right = address((me + 1) % count)

    loads = [
        pltpu.make_async_copy(source, target, load_sem.at[at])
        for at, (source, target) in enumerate(
            (
                (points_hbm, points_ref),
                (charges_hbm, charges_ref),
                (interp_hbm, interp_ref),
                (transfer_hbm, transfer_ref),
                (node_points_hbm, node_points_ref),
                (node_transfer_hbm, node_transfer_ref),
                (far_hbm, far_ref),
            )
        )
    ]
    for load in loads:
        load.start()

    barrier = pltpu.get_barrier_semaphore()
    greeted = 2
    pl.semaphore_signal(barrier, inc=1, device_id=left, device_id_type=MESH)
    pl.semaphore_signal(barrier, inc=1, device_id=right, device_id_type=MESH)
    for name in phases:
        for mask in range(1, size_of[name]):
            pl.semaphore_signal(
                barrier,
                inc=1,
                device_id={name: flipped(where_of[name], mask)},
                device_id_type=MESH,
            )
            greeted += 1

    def unit(n):
        return (
            lax.broadcasted_iota(jnp.int32, (n, n), 0)
            == lax.broadcasted_iota(jnp.int32, (n, n), 1)
        ).astype(jnp.float32)

    eye = unit(rank)

    own_ref[...] = jnp.zeros_like(own_ref)
    pay_ref[...] = jnp.zeros_like(pay_ref)
    loads[0].wait()
    loads[1].wait()
    turned_ref[...] = jnp.concatenate(
        [charges_ref[:, rank:], charges_ref[:, :rank]], axis=1
    )

    def target_step(step, carry):
        for part in range(4):
            leaf = step * 4 + part
            rows = [points_ref[dim, pl.ds(leaf, 1), :] for dim in range(3)]
            rows.append(charges_ref[pl.ds(leaf, 1), :])
            for dim in range(4):
                own_ref[HALO + leaf, dim : dim + 1, :] = rows[dim]
            set_columns(
                column_ref,
                leaf,
                jnp.concatenate(rows + [jnp.zeros((4, pts), jnp.float32)], axis=0),
            )
        return carry

    lax.fori_loop(0, leaves // 4, target_step, 0)

    loads[4].wait()
    for level in range(levels):
        for dim in range(3):
            node_col_ref[3 * level + dim] = jnp.broadcast_to(
                total_lanes(eye * node_points_ref[level, dim]), (rank, rank)
            )

    for load in loads[2:4] + loads[5:]:
        load.wait()

    def skeleton_step(step, acc):
        for part in range(4):
            leaf = step * 4 + part
            upper = turned_ref[pl.ds(leaf, 1), :]
            row = charges_ref[pl.ds(leaf, 1), :]
            col = total_lanes(interp_ref[leaf] * upper[:, :rank] + eye * row[:, :rank])
            own_ref[HALO + leaf, 4:5, 0:rank] = total_rows(eye * col)
            acc = acc + transfer_ref[leaf] * col
        return acc

    acc = lax.fori_loop(0, leaves // 4, skeleton_step, jnp.zeros((rank, rank), jnp.float32))
    node_row = total_rows(acc)

    pl.semaphore_wait(barrier, greeted)
    halo_copies = [
        pltpu.make_async_remote_copy(
            src_ref=own_ref.at[pl.ds(HALO, HALO)],
            dst_ref=win_ref.at[pl.ds(leaves + HALO, HALO)],
            send_sem=halo_send.at[0],
            recv_sem=halo_recv.at[0],
            device_id=left,
            device_id_type=MESH,
        ),
        pltpu.make_async_remote_copy(
            src_ref=own_ref.at[pl.ds(leaves, HALO)],
            dst_ref=win_ref.at[pl.ds(0, HALO)],
            send_sem=halo_send.at[1],
            recv_sem=halo_recv.at[1],
            device_id=right,
            device_id_type=MESH,
        ),
    ]
    for copy in halo_copies:
        copy.start()
    win_ref[HALO : HALO + leaves] = own_ref[HALO : HALO + leaves]

    low_half = lax.broadcasted_iota(jnp.int32, (8, pts), 1) < rank

    def leaf_step(source_ref, leaf):
        place = HALO + leaf
        tx, ty, tz = (own_ref[place, dim : dim + 1, :] for dim in range(3))
        total = jnp.zeros((8, pts), jnp.float32)
        for start in range(0, pts, CHUNK):
            sx, sy, sz, weight = (
                column_ref[leaf, dim, start : start + CHUNK, :] for dim in range(4)
            )
            terms = softened(tx, ty, tz, sx, sy, sz) * weight
            total = total + jnp.sum(terms.reshape(CHUNK // 8, 8, pts), axis=0)
        out_ref[pl.ds(leaf, 1), :] = total_rows(total)
        pairs = []
        for m in range(0, far_slots, 2):
            first = source_ref[far_ref[m, leaf]]
            second = source_ref[far_ref[m + 1, leaf]]
            pairs.append(jnp.where(low_half, first, pltpu.roll(second, rank, 1)))
        for start in range(0, rank, CHUNK):
            tx, ty, tz = (column_ref[leaf, dim, start : start + CHUNK, :] for dim in range(3))
            total = jnp.zeros((CHUNK, pts), jnp.float32)
            for pair in pairs:
                total = total + softened(
                    tx, ty, tz, pair[0:1], pair[1:2], pair[2:3]
                ) * pair[4:5]
            far_acc_ref[leaf, start : start + CHUNK, :] = total

    def run_leaves(source_ref, first, last, place_of=lambda at: at):
        def step(pair, carry):
            leaf_step(source_ref, place_of(first + 2 * pair))
            leaf_step(source_ref, place_of(first + 2 * pair + 1))
            return carry

        lax.fori_loop(0, (last - first) // 2, step, 0)

    def outer(at):
        return at + at // HALO * (leaves - 2 * HALO)

    inner = leaves - 2 * HALO
    level = 0
    pay_at = 0
    recv_at = 0
    for order, name in enumerate(phases):
        bits = size_of[name].bit_length() - 1
        last_phase = order == len(phases) - 1
        chain = [node_row]
        for step in range(bits):
            if last_phase and step == bits - 1:
                chain.append(chain[-1])
            else:
                col = total_lanes(eye * chain[-1])
                chain.append(total_rows(node_transfer_ref[0, level + step] * col))
        for step in range(bits):
            pay_ref[pay_at + step, 0:1, 0:rank] = chain[step]
            for dim in range(3):
                pay_ref[pay_at + step, 1 + dim : 2 + dim, 0:rank] = node_points_ref[
                    level + step, dim
                ]
            pay_ref[pay_at + step, 4:5, 0:rank] = chain[bits]
        copies = []
        for mask in range(1, size_of[name]):
            step = mask.bit_length() - 1
            slot = recv_at + mask - 1
            copy = pltpu.make_async_remote_copy(
                src_ref=pay_ref.at[pay_at + step],
                dst_ref=recv_ref.at[slot],
                send_sem=tree_send.at[slot],
                recv_sem=tree_recv.at[slot],
                device_id={name: flipped(where_of[name], mask)},
                device_id_type=MESH,
            )
            copy.start()
            copies.append(copy)
        if not last_phase:
            spans = max(len(phases) - 1, 1)
            first = HALO + inner * order // spans // 2 * 2
            last = HALO + inner * (order + 1) // spans // 2 * 2
            run_leaves(own_ref, first, last)
        if last_phase:
            for copy in halo_copies:
                copy.wait()

            @pl.when(me == 0)
            def _():
                win_ref[0:HALO] = jnp.zeros((HALO, 8, pts), jnp.float32)

            @pl.when(me == count - 1)
            def _():
                win_ref[leaves + HALO :] = jnp.zeros((HALO, 8, pts), jnp.float32)

            run_leaves(win_ref, 0, 2 * HALO, outer)
        for copy in copies:
            copy.wait()
        node_row = chain[bits]
        for mask in range(1, size_of[name]):
            node_row = node_row + recv_ref[recv_at + mask - 1, 4:5, 0:rank]
        for step in range(bits):
            base = recv_at + 2**step - 1
            sibling = recv_ref[base, 0:1, 0:rank]
            for other in range(1, 2**step):
                sibling = sibling + recv_ref[base + other, 0:1, 0:rank]
            targets = [node_col_ref[3 * (level + step) + dim] for dim in range(3)]
            sources = [recv_ref[base, 1 + dim : 2 + dim, 0:rank] for dim in range(3)]
            coupling_ref[level + step] = softened(*targets, *sources) * sibling
        level += bits
        pay_at += bits
        recv_at += size_of[name] - 1

    expansion = total_lanes(coupling_ref[levels - 1])
    for level in range(levels - 2, -1, -1):
        expansion = total_lanes(
            coupling_ref[level] + node_transfer_ref[0, level] * total_rows(eye * expansion)
        )
    expansion_row = total_rows(eye * expansion)

    def finish_step(step, carry):
        for part in range(4):
            leaf = step * 4 + part
            combined = total_lanes(transfer_ref[leaf] * expansion_row) + total_lanes(
                far_acc_ref[leaf]
            )
            row = jnp.concatenate(
                [total_rows(eye * combined), total_rows(interp_ref[leaf] * combined)], axis=1
            )
            out_ref[pl.ds(leaf, 1), :] = out_ref[pl.ds(leaf, 1), :] + row
        return carry

    lax.fori_loop(0, leaves // 4, finish_step, 0)


def near_body(
    near_hbm,
    count_hbm,
    part_hbm,
    win_hbm,
    out_ref,
    near_ref,
    count_ref,
    part_ref,
    win_ref,
    column_ref,
    sem,
):
    loads = [
        pltpu.make_async_copy(source, target, sem.at[at])
        for at, (source, target) in enumerate(
            (
                (win_hbm, win_ref),
                (near_hbm, near_ref),
                (count_hbm, count_ref),
                (part_hbm, part_ref),
            )
        )
    ]
    for load in loads:
        load.start()
    loads[0].wait()

    def column_step(step, carry):
        for part in range(4):
            set_columns(column_ref, step * 4 + part, win_ref[step * 4 + part])
        return carry

    lax.fori_loop(0, win_ref.shape[0] // 4, column_step, 0)
    for load in loads[1:]:
        load.wait()
    slots, leaves = near_ref.shape
    pts = part_ref.shape[1]

    def leaf_step(leaf, carry):
        live = count_ref[leaf]
        tx, ty, tz = (
            jnp.broadcast_to(win_ref[HALO + leaf, dim : dim + 1, :], (8, pts)) for dim in range(3)
        )

        def terms(slot):
            place = near_ref[jnp.minimum(slot, slots - 1), leaf]
            total = jnp.zeros((8, pts), jnp.float32)
            for start in range(0, pts, 8):
                sx, sy, sz, weight = (
                    column_ref[place, dim, start : start + 8, :] for dim in range(4)
                )
                total = total + softened(tx, ty, tz, sx, sy, sz) * weight
            return total

        def pair_step(pair, acc):
            second = 2 * pair + 2
            return acc + terms(second - 1) + jnp.where(second < live, terms(second), 0.0)

        acc = lax.fori_loop(0, live // 2, pair_step, jnp.zeros((8, pts), jnp.float32))
        out_ref[pl.ds(leaf, 1), :] = part_ref[pl.ds(leaf, 1), :] + total_rows(acc)
        return carry

    lax.fori_loop(0, leaves, leaf_step, 0)


def on_device(
    sizes,
    points,
    charges,
    interpolant,
    leaf_transfer,
    node_transfer,
    node_points,
    near_list,
    near_count,
    far_list,
):
    points = points.transpose(1, 0, 2)
    node_points = node_points.transpose(1, 2, 0, 3)
    near_list = near_list.T
    far_list = far_list.T
    leaves, pts = charges.shape
    rank = interpolant.shape[1]
    levels = node_transfer.shape[1]
    peers = sum(size - 1 for size in sizes)
    vmem = pl.BlockSpec(memory_space=pltpu.VMEM)
    hbm = pl.BlockSpec(memory_space=pltpu.HBM)
    f32 = jnp.float32
    window = leaves + 2 * HALO
    part, win = pl.pallas_call(
        functools.partial(body, sizes),
        out_shape=[
            jax.ShapeDtypeStruct(charges.shape, f32),
            jax.ShapeDtypeStruct((window, 8, pts), f32),
        ],
        in_specs=[hbm] * 7,
        out_specs=[vmem] * 2,
        scratch_shapes=[
            pltpu.SMEM(far_list.shape, jnp.int32),
            pltpu.VMEM(points.shape, f32),
            pltpu.VMEM(charges.shape, f32),
            pltpu.VMEM(interpolant.shape, f32),
            pltpu.VMEM(leaf_transfer.shape, f32),
            pltpu.VMEM(node_transfer.shape, f32),
            pltpu.VMEM(node_points.shape, f32),
            pltpu.VMEM(charges.shape, f32),
            pltpu.VMEM((window, 8, pts), f32),
            pltpu.VMEM((leaves, 4, pts, pts), f32),
            pltpu.VMEM((leaves, rank, pts), f32),
            pltpu.VMEM((levels, rank, rank), f32),
            pltpu.VMEM((3 * levels, rank, rank), f32),
            pltpu.VMEM((levels, 8, pts), f32),
            pltpu.VMEM((peers, 8, pts), f32),
            pltpu.SemaphoreType.DMA((7,)),
            pltpu.SemaphoreType.DMA((2,)),
            pltpu.SemaphoreType.DMA((2,)),
            pltpu.SemaphoreType.DMA((peers,)),
            pltpu.SemaphoreType.DMA((peers,)),
        ],
        compiler_params=pltpu.CompilerParams(
            collective_id=0, has_side_effects=True, vmem_limit_bytes=63 * 2**20
        ),
    )(
        far_list,
        points,
        charges,
        interpolant,
        leaf_transfer,
        node_transfer,
        node_points,
    )
    return pl.pallas_call(
        near_body,
        out_shape=jax.ShapeDtypeStruct(charges.shape, f32),
        in_specs=[hbm] * 4,
        out_specs=vmem,
        scratch_shapes=[
            pltpu.SMEM(near_list.shape, jnp.int32),
            pltpu.SMEM(near_count.shape, jnp.int32),
            pltpu.VMEM(charges.shape, f32),
            pltpu.VMEM((window, 8, pts), f32),
            pltpu.VMEM((window, 4, pts, pts), f32),
            pltpu.SemaphoreType.DMA((4,)),
        ],
        compiler_params=pltpu.CompilerParams(vmem_limit_bytes=63 * 2**20),
    )(near_list, near_count, part, win)


def solution(mesh):
    sizes = tuple(mesh.shape[name] for name in AXES)
    return jax.shard_map(
        functools.partial(on_device, sizes),
        mesh=mesh,
        in_specs=(
            P(AXES, None, None),
            P(AXES, None),
            P(AXES, None, None),
            P(AXES, None, None),
            P(AXES, None, None, None),
            P(AXES, None, None, None),
            P(AXES, None),
            P(AXES),
            P(AXES, None),
        ),
        out_specs=P(AXES, None),
        check_vma=False,
    )
```

```python
import functools
import math

import jax
import jax.numpy as jnp
from jax import lax
from jax.experimental import pallas as pl
from jax.experimental.pallas import tpu as pltpu
from jax.sharding import PartitionSpec as P

HALO = 8
SOFTENING = 0.0625
MESH = pl.DeviceIdType.MESH
AXES = ("gx", "gy", "gz")
CHUNK = 32
GROUP = 8


def flipped(place, mask):
    result = place
    bit = 1
    while bit <= mask:
        if mask & bit:
            result = result + bit - 2 * bit * ((place // bit) % 2)
        bit *= 2
    return result


def total_lanes(value):
    return jnp.sum(value, axis=1, keepdims=True)


def total_rows(value):
    return jnp.sum(value, axis=0, keepdims=True)


def softened(tx, ty, tz, sx, sy, sz):
    dx = tx - sx
    dy = ty - sy
    dz = tz - sz
    return lax.rsqrt(dx * dx + dy * dy + dz * dz + SOFTENING)


def body(
    sizes,
    near_hbm,
    count_hbm,
    far_hbm,
    points_hbm,
    charges_hbm,
    interp_hbm,
    transfer_hbm,
    node_transfer_hbm,
    node_points_hbm,
    out_ref,
    far_out_ref,
    near_ref,
    count_ref,
    far_ref,
    points_ref,
    charges_ref,
    interp_ref,
    transfer_ref,
    node_transfer_ref,
    node_points_ref,
    turned_ref,
    own_ref,
    win_ref,
    column_ref,
    far_acc_ref,
    coupling_ref,
    node_col_ref,
    pay_ref,
    recv_ref,
    load_sem,
    halo_send,
    halo_recv,
    tree_send,
    tree_recv,
):
    leaves, pts = charges_ref.shape
    rank = interp_ref.shape[1]
    near_slots = near_ref.shape[0]
    far_slots = far_ref.shape[0]
    levels = node_transfer_ref.shape[1]
    gx, gy, gz = (lax.axis_index(name) for name in AXES)
    nx, ny, nz = sizes
    count = nx * ny * nz
    me = (gx * ny + gy) * nz + gz
    where_of = {"gx": gx, "gy": gy, "gz": gz}
    size_of = dict(zip(AXES, sizes))
    phases = []
    for name in ("gz", "gy", "gx"):
        if size_of[name] == 1:
            continue
        if phases and math.prod(size_of[x] for x in phases[-1]) * size_of[name] <= GROUP:
            phases[-1].append(name)
        else:
            phases.append([name])
    extents = [math.prod(size_of[x] for x in names) for names in phases]

    def peer(names, mask):
        found = {}
        for axis in names:
            part = mask % size_of[axis]
            mask //= size_of[axis]
            if part:
                found[axis] = flipped(where_of[axis], part)
        return found

    def address(index):
        return {
            "gx": index // (ny * nz),
            "gy": (index // nz) % ny,
            "gz": index % nz,
        }

    left = address((me + count - 1) % count)
    right = address((me + 1) % count)

    loads = [
        pltpu.make_async_copy(source, target, load_sem.at[at])
        for at, (source, target) in enumerate(
            (
                (points_hbm, points_ref),
                (charges_hbm, charges_ref),
                (interp_hbm, interp_ref),
                (transfer_hbm, transfer_ref),
                (node_points_hbm, node_points_ref),
                (node_transfer_hbm, node_transfer_ref),
                (near_hbm, near_ref),
                (count_hbm, count_ref),
                (far_hbm, far_ref),
            )
        )
    ]
    for load in loads:
        load.start()

    barrier = pltpu.get_barrier_semaphore()
    greeted = 2
    pl.semaphore_signal(barrier, inc=1, device_id=left, device_id_type=MESH)
    pl.semaphore_signal(barrier, inc=1, device_id=right, device_id_type=MESH)
    for names, extent in zip(phases, extents):
        for mask in range(1, extent):
            pl.semaphore_signal(
                barrier,
                inc=1,
                device_id=peer(names, mask),
                device_id_type=MESH,
            )
            greeted += 1

    def unit(n):
        return (
            lax.broadcasted_iota(jnp.int32, (n, n), 0)
            == lax.broadcasted_iota(jnp.int32, (n, n), 1)
        ).astype(jnp.float32)

    eye = unit(rank)
    eye_pts = unit(pts)

    own_ref[...] = jnp.zeros_like(own_ref)
    pay_ref[...] = jnp.zeros_like(pay_ref)
    loads[0].wait()
    loads[1].wait()
    turned_ref[...] = jnp.concatenate(
        [charges_ref[:, rank:], charges_ref[:, :rank]], axis=1
    )

    for load in loads[2:]:
        load.wait()

    def skeleton_step(step, acc):
        for part in range(8):
            leaf = step * 8 + part
            upper = turned_ref[pl.ds(leaf, 1), :]
            row = charges_ref[pl.ds(leaf, 1), :]
            col = total_lanes(interp_ref[leaf] * upper[:, :rank] + eye * row[:, :rank])
            for dim in range(3):
                own_ref[HALO + leaf, dim : dim + 1, :] = points_ref[dim, pl.ds(leaf, 1), :]
            own_ref[HALO + leaf, 3:4, :] = row
            own_ref[HALO + leaf, 4:5, 0:rank] = total_rows(eye * col)
            acc = acc + transfer_ref[leaf] * col
        return acc

    acc = lax.fori_loop(0, leaves // 8, skeleton_step, jnp.zeros((rank, rank), jnp.float32))
    node_row = total_rows(acc)
    halo_copies = [
        pltpu.make_async_remote_copy(
            src_ref=own_ref.at[pl.ds(HALO, HALO)],
            dst_ref=win_ref.at[pl.ds(leaves + HALO, HALO)],
            send_sem=halo_send.at[0],
            recv_sem=halo_recv.at[0],
            device_id=left,
            device_id_type=MESH,
        ),
        pltpu.make_async_remote_copy(
            src_ref=own_ref.at[pl.ds(leaves, HALO)],
            dst_ref=win_ref.at[pl.ds(0, HALO)],
            send_sem=halo_send.at[1],
            recv_sem=halo_recv.at[1],
            device_id=right,
            device_id_type=MESH,
        ),
    ]
    def while_first_travels():
        for copy in halo_copies:
            copy.start()
        win_ref[HALO : HALO + leaves] = own_ref[HALO : HALO + leaves]
        def target_step(step, carry):
            for part in range(4):
                leaf = step * 4 + part
                rows = [points_ref[dim, pl.ds(leaf, 1), :] for dim in range(3)]
                tile = jnp.transpose(jnp.concatenate(rows + [jnp.zeros((5, pts), jnp.float32)], axis=0))
                for dim in range(3):
                    column_ref[leaf, dim] = jnp.broadcast_to(tile[:, dim : dim + 1], (pts, pts))
            return carry

        lax.fori_loop(0, leaves // 4, target_step, 0)

        for level in range(levels):
            for dim in range(3):
                node_col_ref[3 * level + dim] = jnp.broadcast_to(
                    total_lanes(eye * node_points_ref[level, dim]), (rank, rank)
                )

    low_half = lax.broadcasted_iota(jnp.int32, (8, pts), 1) < rank

    def leaf_step(source_ref, leaf):
        live = count_ref[leaf]
        places = [near_ref[m, leaf] for m in range(near_slots)]
        weights = [
            jnp.where(m < live, source_ref[places[m], 3:4, :], 0.0) for m in range(near_slots)
        ]
        near_cols = []
        for start in range(0, pts, CHUNK):
            tx, ty, tz = (column_ref[leaf, dim, start : start + CHUNK, :] for dim in range(3))
            total = jnp.zeros((CHUNK, pts), jnp.float32)
            for m in range(near_slots):
                sx, sy, sz = (source_ref[places[m], dim : dim + 1, :] for dim in range(3))
                total = total + softened(tx, ty, tz, sx, sy, sz) * weights[m]
            near_cols.append(total_lanes(total))
        near_col = jnp.concatenate(near_cols, axis=0)
        out_ref[pl.ds(leaf, 1), :] = total_rows(eye_pts * near_col)
        pairs = []
        for m in range(0, far_slots, 2):
            first = source_ref[far_ref[m, leaf]]
            second = source_ref[far_ref[m + 1, leaf]]
            pairs.append(jnp.where(low_half, first, pltpu.roll(second, rank, 1)))
        for start in range(0, rank, CHUNK):
            tx, ty, tz = (column_ref[leaf, dim, start : start + CHUNK, :] for dim in range(3))
            total = jnp.zeros((CHUNK, pts), jnp.float32)
            for pair in pairs:
                total = total + softened(
                    tx, ty, tz, pair[0:1], pair[1:2], pair[2:3]
                ) * pair[4:5]
            far_acc_ref[leaf, start : start + CHUNK, :] = total

    def run_leaves(source_ref, first, last):
        def step(pair, carry):
            leaf_step(source_ref, first + 2 * pair)
            leaf_step(source_ref, first + 2 * pair + 1)
            return carry

        lax.fori_loop(0, (last - first) // 2, step, 0)

    inner = leaves - 2 * HALO
    level = 0
    pay_at = 0
    recv_at = 0
    for order, (names, extent) in enumerate(zip(phases, extents)):
        bits = extent.bit_length() - 1
        last_phase = order == len(phases) - 1
        chain = [node_row]
        for step in range(bits):
            if last_phase and step == bits - 1:
                chain.append(chain[-1])
            else:
                col = total_lanes(eye * chain[-1])
                chain.append(total_rows(node_transfer_ref[0, level + step] * col))
        for step in range(bits):
            pay_ref[pay_at + step, 0:1, 0:rank] = chain[step]
            for dim in range(3):
                pay_ref[pay_at + step, 1 + dim : 2 + dim, 0:rank] = node_points_ref[
                    level + step, dim
                ]
            pay_ref[pay_at + step, 4:5, 0:rank] = chain[bits]
        if order == 0:
            pl.semaphore_wait(barrier, greeted)
        copies = []
        for mask in range(1, extent):
            step = mask.bit_length() - 1
            slot = recv_at + mask - 1
            copy = pltpu.make_async_remote_copy(
                src_ref=pay_ref.at[pay_at + step],
                dst_ref=recv_ref.at[slot],
                send_sem=tree_send.at[slot],
                recv_sem=tree_recv.at[slot],
                device_id=peer(names, mask),
                device_id_type=MESH,
            )
            copy.start()
            copies.append(copy)
        if order == 0:
            while_first_travels()
        spans = max(len(phases) - 1, 1)
        if order < spans:
            first = HALO + inner * order // spans // 2 * 2
            last = HALO + inner * (order + 1) // spans // 2 * 2
            run_leaves(own_ref, first, last)
        if last_phase:
            for copy in halo_copies:
                copy.wait()

            @pl.when(me == 0)
            def _():
                win_ref[0:HALO] = jnp.zeros((HALO, 8, pts), jnp.float32)

            @pl.when(me == count - 1)
            def _():
                win_ref[leaves + HALO :] = jnp.zeros((HALO, 8, pts), jnp.float32)

            run_leaves(win_ref, 0, HALO)
            run_leaves(win_ref, leaves - HALO, leaves)
        for copy in copies:
            copy.wait()
        node_row = chain[bits]
        for mask in range(1, extent):
            node_row = node_row + recv_ref[recv_at + mask - 1, 4:5, 0:rank]
        for step in range(bits):
            base = recv_at + 2**step - 1
            sibling = recv_ref[base, 0:1, 0:rank]
            for other in range(1, 2**step):
                sibling = sibling + recv_ref[base + other, 0:1, 0:rank]
            targets = [node_col_ref[3 * (level + step) + dim] for dim in range(3)]
            sources = [recv_ref[base, 1 + dim : 2 + dim, 0:rank] for dim in range(3)]
            coupling_ref[level + step] = softened(*targets, *sources) * sibling
        level += bits
        pay_at += bits
        recv_at += extent - 1

    expansion = total_lanes(coupling_ref[levels - 1])
    for level in range(levels - 2, -1, -1):
        expansion = total_lanes(
            coupling_ref[level] + node_transfer_ref[0, level] * total_rows(eye * expansion)
        )
    expansion_row = total_rows(eye * expansion)

    def finish_step(step, carry):
        for part in range(8):
            leaf = step * 8 + part
            combined = total_lanes(transfer_ref[leaf] * expansion_row) + total_lanes(
                far_acc_ref[leaf]
            )
            row = jnp.concatenate(
                [total_rows(eye * combined), total_rows(interp_ref[leaf] * combined)], axis=1
            )
            far_out_ref[pl.ds(leaf, 1), :] = row
        return carry

    lax.fori_loop(0, leaves // 8, finish_step, 0)


def on_device(
    sizes,
    points,
    charges,
    interpolant,
    leaf_transfer,
    node_transfer,
    node_points,
    near_list,
    near_count,
    far_list,
):
    points = points.transpose(1, 0, 2)
    node_points = node_points.transpose(1, 2, 0, 3)
    near_list = near_list.T
    far_list = far_list.T
    leaves, pts = charges.shape
    rank = interpolant.shape[1]
    levels = node_transfer.shape[1]
    peers = math.prod(sizes) - 1
    vmem = pl.BlockSpec(memory_space=pltpu.VMEM)
    hbm = pl.BlockSpec(memory_space=pl.ANY)
    f32 = jnp.float32
    near_part, far_part = pl.pallas_call(
        functools.partial(body, sizes),
        out_shape=[jax.ShapeDtypeStruct(charges.shape, f32)] * 2,
        in_specs=[hbm] * 9,
        out_specs=[vmem] * 2,
        scratch_shapes=[
            pltpu.SMEM(near_list.shape, jnp.int32),
            pltpu.SMEM(near_count.shape, jnp.int32),
            pltpu.SMEM(far_list.shape, jnp.int32),
            pltpu.VMEM(points.shape, f32),
            pltpu.VMEM(charges.shape, f32),
            pltpu.VMEM(interpolant.shape, f32),
            pltpu.VMEM(leaf_transfer.shape, f32),
            pltpu.VMEM(node_transfer.shape, f32),
            pltpu.VMEM(node_points.shape, f32),
            pltpu.VMEM(charges.shape, f32),
            pltpu.VMEM((leaves + 2 * HALO, 8, pts), f32),
            pltpu.VMEM((leaves + 2 * HALO, 8, pts), f32),
            pltpu.VMEM((leaves, 3, pts, pts), f32),
            pltpu.VMEM((leaves, rank, pts), f32),
            pltpu.VMEM((levels, rank, rank), f32),
            pltpu.VMEM((3 * levels, rank, rank), f32),
            pltpu.VMEM((levels, 8, pts), f32),
            pltpu.VMEM((peers, 8, pts), f32),
            pltpu.SemaphoreType.DMA((9,)),
            pltpu.SemaphoreType.DMA((2,)),
            pltpu.SemaphoreType.DMA((2,)),
            pltpu.SemaphoreType.DMA((peers,)),
            pltpu.SemaphoreType.DMA((peers,)),
        ],
        compiler_params=pltpu.CompilerParams(
            collective_id=0, has_side_effects=True, vmem_limit_bytes=63 * 2**20
        ),
    )(
        near_list,
        near_count,
        far_list,
        points,
        charges,
        interpolant,
        leaf_transfer,
        node_transfer,
        node_points,
    )
    return near_part + far_part


def solution(mesh):
    sizes = tuple(mesh.shape[name] for name in AXES)
    return jax.shard_map(
        functools.partial(on_device, sizes),
        mesh=mesh,
        in_specs=(
            P(AXES, None, None),
            P(AXES, None),
            P(AXES, None, None),
            P(AXES, None, None),
            P(AXES, None, None, None),
            P(AXES, None, None, None),
            P(AXES, None),
            P(AXES),
            P(AXES, None),
        ),
        out_specs=P(AXES, None),
        check_vma=False,
    )
```

```python
import functools
import math

import jax
import jax.numpy as jnp
from jax import lax
from jax.experimental import pallas as pl
from jax.experimental.pallas import tpu as pltpu
from jax.sharding import PartitionSpec as P

HALO = 8
SOFTENING = 0.0625
MESH = pl.DeviceIdType.MESH
AXES = ("gx", "gy", "gz")
CHUNK = 32
GROUP = 8


def flipped(place, mask):
    result = place
    bit = 1
    while bit <= mask:
        if mask & bit:
            result = result + bit - 2 * bit * ((place // bit) % 2)
        bit *= 2
    return result


def total_lanes(value):
    return jnp.sum(value, axis=1, keepdims=True)


def total_rows(value):
    return jnp.sum(value, axis=0, keepdims=True)


def softened(tx, ty, tz, sx, sy, sz):
    dx = tx - sx
    dy = ty - sy
    dz = tz - sz
    return lax.rsqrt(dx * dx + dy * dy + dz * dz + SOFTENING)


def body(
    sizes,
    near_hbm,
    count_hbm,
    far_hbm,
    points_hbm,
    charges_hbm,
    interp_hbm,
    transfer_hbm,
    node_transfer_hbm,
    node_points_hbm,
    out_ref,
    far_out_ref,
    near_ref,
    count_ref,
    far_ref,
    points_ref,
    charges_ref,
    interp_ref,
    transfer_ref,
    node_transfer_ref,
    node_points_ref,
    turned_ref,
    own_ref,
    win_ref,
    column_ref,
    far_acc_ref,
    coupling_ref,
    node_col_ref,
    pay_ref,
    recv_ref,
    load_sem,
    halo_send,
    halo_recv,
    tree_send,
    tree_recv,
):
    leaves, pts = charges_ref.shape
    rank = interp_ref.shape[1]
    near_slots = near_ref.shape[0]
    far_slots = far_ref.shape[0]
    levels = node_transfer_ref.shape[1]
    gx, gy, gz = (lax.axis_index(name) for name in AXES)
    nx, ny, nz = sizes
    count = nx * ny * nz
    me = (gx * ny + gy) * nz + gz
    where_of = {"gx": gx, "gy": gy, "gz": gz}
    size_of = dict(zip(AXES, sizes))
    phases = []
    for name in ("gz", "gy", "gx"):
        if size_of[name] == 1:
            continue
        if phases and math.prod(size_of[x] for x in phases[-1]) * size_of[name] <= GROUP:
            phases[-1].append(name)
        else:
            phases.append([name])
    extents = [math.prod(size_of[x] for x in names) for names in phases]

    def peer(names, mask):
        found = {}
        for axis in names:
            part = mask % size_of[axis]
            mask //= size_of[axis]
            if part:
                found[axis] = flipped(where_of[axis], part)
        return found

    def address(index):
        return {
            "gx": index // (ny * nz),
            "gy": (index // nz) % ny,
            "gz": index % nz,
        }

    left = address((me + count - 1) % count)
    right = address((me + 1) % count)

    loads = [
        pltpu.make_async_copy(source, target, load_sem.at[at])
        for at, (source, target) in enumerate(
            (
                (points_hbm, points_ref),
                (charges_hbm, charges_ref),
                (interp_hbm, interp_ref),
                (transfer_hbm, transfer_ref),
                (node_points_hbm, node_points_ref),
                (node_transfer_hbm, node_transfer_ref),
                (near_hbm, near_ref),
                (count_hbm, count_ref),
                (far_hbm, far_ref),
            )
        )
    ]
    for load in loads:
        load.start()

    barrier = pltpu.get_barrier_semaphore()
    greeted = 2
    pl.semaphore_signal(barrier, inc=1, device_id=left, device_id_type=MESH)
    pl.semaphore_signal(barrier, inc=1, device_id=right, device_id_type=MESH)
    for names, extent in zip(phases, extents):
        for mask in range(1, extent):
            pl.semaphore_signal(
                barrier,
                inc=1,
                device_id=peer(names, mask),
                device_id_type=MESH,
            )
            greeted += 1

    def unit(n):
        return (
            lax.broadcasted_iota(jnp.int32, (n, n), 0)
            == lax.broadcasted_iota(jnp.int32, (n, n), 1)
        ).astype(jnp.float32)

    eye = unit(rank)
    eye_pts = unit(pts)

    own_ref[...] = jnp.zeros_like(own_ref)
    pay_ref[...] = jnp.zeros_like(pay_ref)
    loads[0].wait()
    loads[1].wait()
    turned_ref[...] = jnp.concatenate(
        [charges_ref[:, rank:], charges_ref[:, :rank]], axis=1
    )

    def target_step(step, carry):
        for part in range(4):
            leaf = step * 4 + part
            rows = [points_ref[dim, pl.ds(leaf, 1), :] for dim in range(3)]
            tile = jnp.transpose(jnp.concatenate(rows + [jnp.zeros((5, pts), jnp.float32)], axis=0))
            for dim in range(3):
                column_ref[leaf, dim] = jnp.broadcast_to(tile[:, dim : dim + 1], (pts, pts))
        return carry

    lax.fori_loop(0, leaves // 4, target_step, 0)

    loads[4].wait()
    for level in range(levels):
        for dim in range(3):
            node_col_ref[3 * level + dim] = jnp.broadcast_to(
                total_lanes(eye * node_points_ref[level, dim]), (rank, rank)
            )

    for load in loads[2:4] + loads[5:]:
        load.wait()

    def skeleton_step(step, acc):
        for part in range(8):
            leaf = step * 8 + part
            upper = turned_ref[pl.ds(leaf, 1), :]
            row = charges_ref[pl.ds(leaf, 1), :]
            col = total_lanes(interp_ref[leaf] * upper[:, :rank] + eye * row[:, :rank])
            for dim in range(3):
                own_ref[HALO + leaf, dim : dim + 1, :] = points_ref[dim, pl.ds(leaf, 1), :]
            own_ref[HALO + leaf, 3:4, :] = row
            own_ref[HALO + leaf, 4:5, 0:rank] = total_rows(eye * col)
            acc = acc + transfer_ref[leaf] * col
        return acc

    acc = lax.fori_loop(0, leaves // 8, skeleton_step, jnp.zeros((rank, rank), jnp.float32))
    node_row = total_rows(acc)
    halo_copies = [
        pltpu.make_async_remote_copy(
            src_ref=own_ref.at[pl.ds(HALO, HALO)],
            dst_ref=win_ref.at[pl.ds(leaves + HALO, HALO)],
            send_sem=halo_send.at[0],
            recv_sem=halo_recv.at[0],
            device_id=left,
            device_id_type=MESH,
        ),
        pltpu.make_async_remote_copy(
            src_ref=own_ref.at[pl.ds(leaves, HALO)],
            dst_ref=win_ref.at[pl.ds(0, HALO)],
            send_sem=halo_send.at[1],
            recv_sem=halo_recv.at[1],
            device_id=right,
            device_id_type=MESH,
        ),
    ]
    def while_first_travels():
        for copy in halo_copies:
            copy.start()
        win_ref[HALO : HALO + leaves] = own_ref[HALO : HALO + leaves]

    low_half = lax.broadcasted_iota(jnp.int32, (8, pts), 1) < rank

    def leaf_step(source_ref, leaf):
        live = count_ref[leaf]
        places = [near_ref[m, leaf] for m in range(near_slots)]
        weights = [
            jnp.where(m < live, source_ref[places[m], 3:4, :], 0.0) for m in range(near_slots)
        ]
        near_cols = []
        for start in range(0, pts, CHUNK):
            tx, ty, tz = (column_ref[leaf, dim, start : start + CHUNK, :] for dim in range(3))
            total = jnp.zeros((CHUNK, pts), jnp.float32)
            for m in range(near_slots):
                sx, sy, sz = (source_ref[places[m], dim : dim + 1, :] for dim in range(3))
                total = total + softened(tx, ty, tz, sx, sy, sz) * weights[m]
            near_cols.append(total_lanes(total))
        near_col = jnp.concatenate(near_cols, axis=0)
        out_ref[pl.ds(leaf, 1), :] = total_rows(eye_pts * near_col)
        pairs = []
        for m in range(0, far_slots, 2):
            first = source_ref[far_ref[m, leaf]]
            second = source_ref[far_ref[m + 1, leaf]]
            pairs.append(jnp.where(low_half, first, pltpu.roll(second, rank, 1)))
        for start in range(0, rank, CHUNK):
            tx, ty, tz = (column_ref[leaf, dim, start : start + CHUNK, :] for dim in range(3))
            total = jnp.zeros((CHUNK, pts), jnp.float32)
            for pair in pairs:
                total = total + softened(
                    tx, ty, tz, pair[0:1], pair[1:2], pair[2:3]
                ) * pair[4:5]
            far_acc_ref[leaf, start : start + CHUNK, :] = total

    def run_leaves(source_ref, first, last):
        def step(pair, carry):
            leaf_step(source_ref, first + 2 * pair)
            leaf_step(source_ref, first + 2 * pair + 1)
            return carry

        lax.fori_loop(0, (last - first) // 2, step, 0)

    inner = leaves - 2 * HALO
    level = 0
    pay_at = 0
    recv_at = 0
    for order, (names, extent) in enumerate(zip(phases, extents)):
        bits = extent.bit_length() - 1
        last_phase = order == len(phases) - 1
        chain = [node_row]
        for step in range(bits):
            if last_phase and step == bits - 1:
                chain.append(chain[-1])
            else:
                col = total_lanes(eye * chain[-1])
                chain.append(total_rows(node_transfer_ref[0, level + step] * col))
        for step in range(bits):
            pay_ref[pay_at + step, 0:1, 0:rank] = chain[step]
            for dim in range(3):
                pay_ref[pay_at + step, 1 + dim : 2 + dim, 0:rank] = node_points_ref[
                    level + step, dim
                ]
            pay_ref[pay_at + step, 4:5, 0:rank] = chain[bits]
        if order == 0:
            pl.semaphore_wait(barrier, greeted)
        copies = []
        for mask in range(1, extent):
            step = mask.bit_length() - 1
            slot = recv_at + mask - 1
            copy = pltpu.make_async_remote_copy(
                src_ref=pay_ref.at[pay_at + step],
                dst_ref=recv_ref.at[slot],
                send_sem=tree_send.at[slot],
                recv_sem=tree_recv.at[slot],
                device_id=peer(names, mask),
                device_id_type=MESH,
            )
            copy.start()
            copies.append(copy)
        if order == 0:
            while_first_travels()
        spans = max(len(phases) - 1, 1)
        if order < spans:
            first = HALO + inner * order // spans // 2 * 2
            last = HALO + inner * (order + 1) // spans // 2 * 2
            run_leaves(own_ref, first, last)
        if last_phase:
            for copy in halo_copies:
                copy.wait()

            @pl.when(me == 0)
            def _():
                win_ref[0:HALO] = jnp.zeros((HALO, 8, pts), jnp.float32)

            @pl.when(me == count - 1)
            def _():
                win_ref[leaves + HALO :] = jnp.zeros((HALO, 8, pts), jnp.float32)

            run_leaves(win_ref, 0, HALO)
            run_leaves(win_ref, leaves - HALO, leaves)
        for copy in copies:
            copy.wait()
        node_row = chain[bits]
        for mask in range(1, extent):
            node_row = node_row + recv_ref[recv_at + mask - 1, 4:5, 0:rank]
        for step in range(bits):
            base = recv_at + 2**step - 1
            sibling = recv_ref[base, 0:1, 0:rank]
            for other in range(1, 2**step):
                sibling = sibling + recv_ref[base + other, 0:1, 0:rank]
            targets = [node_col_ref[3 * (level + step) + dim] for dim in range(3)]
            sources = [recv_ref[base, 1 + dim : 2 + dim, 0:rank] for dim in range(3)]
            coupling_ref[level + step] = softened(*targets, *sources) * sibling
        level += bits
        pay_at += bits
        recv_at += extent - 1

    expansion = total_lanes(coupling_ref[levels - 1])
    for level in range(levels - 2, -1, -1):
        expansion = total_lanes(
            coupling_ref[level] + node_transfer_ref[0, level] * total_rows(eye * expansion)
        )
    expansion_row = total_rows(eye * expansion)

    def finish_step(step, carry):
        for part in range(8):
            leaf = step * 8 + part
            combined = total_lanes(transfer_ref[leaf] * expansion_row) + total_lanes(
                far_acc_ref[leaf]
            )
            row = jnp.concatenate(
                [total_rows(eye * combined), total_rows(interp_ref[leaf] * combined)], axis=1
            )
            far_out_ref[pl.ds(leaf, 1), :] = row
        return carry

    lax.fori_loop(0, leaves // 8, finish_step, 0)


def on_device(
    sizes,
    points,
    charges,
    interpolant,
    leaf_transfer,
    node_transfer,
    node_points,
    near_list,
    near_count,
    far_list,
):
    points = points.transpose(1, 0, 2)
    node_points = node_points.transpose(1, 2, 0, 3)
    near_list = near_list.T
    far_list = far_list.T
    leaves, pts = charges.shape
    rank = interpolant.shape[1]
    levels = node_transfer.shape[1]
    peers = math.prod(sizes) - 1
    vmem = pl.BlockSpec(memory_space=pltpu.VMEM)
    hbm = pl.BlockSpec(memory_space=pl.ANY)
    f32 = jnp.float32
    near_part, far_part = pl.pallas_call(
        functools.partial(body, sizes),
        out_shape=[jax.ShapeDtypeStruct(charges.shape, f32)] * 2,
        in_specs=[hbm] * 9,
        out_specs=[vmem] * 2,
        scratch_shapes=[
            pltpu.SMEM(near_list.shape, jnp.int32),
            pltpu.SMEM(near_count.shape, jnp.int32),
            pltpu.SMEM(far_list.shape, jnp.int32),
            pltpu.VMEM(points.shape, f32),
            pltpu.VMEM(charges.shape, f32),
            pltpu.VMEM(interpolant.shape, f32),
            pltpu.VMEM(leaf_transfer.shape, f32),
            pltpu.VMEM(node_transfer.shape, f32),
            pltpu.VMEM(node_points.shape, f32),
            pltpu.VMEM(charges.shape, f32),
            pltpu.VMEM((leaves + 2 * HALO, 8, pts), f32),
            pltpu.VMEM((leaves + 2 * HALO, 8, pts), f32),
            pltpu.VMEM((leaves, 3, pts, pts), f32),
            pltpu.VMEM((leaves, rank, pts), f32),
            pltpu.VMEM((levels, rank, rank), f32),
            pltpu.VMEM((3 * levels, rank, rank), f32),
            pltpu.VMEM((levels, 8, pts), f32),
            pltpu.VMEM((peers, 8, pts), f32),
            pltpu.SemaphoreType.DMA((9,)),
            pltpu.SemaphoreType.DMA((2,)),
            pltpu.SemaphoreType.DMA((2,)),
            pltpu.SemaphoreType.DMA((peers,)),
            pltpu.SemaphoreType.DMA((peers,)),
        ],
        compiler_params=pltpu.CompilerParams(
            collective_id=0, has_side_effects=True, vmem_limit_bytes=63 * 2**20
        ),
    )(
        near_list,
        near_count,
        far_list,
        points,
        charges,
        interpolant,
        leaf_transfer,
        node_transfer,
        node_points,
    )
    return near_part + far_part


def solution(mesh):
    sizes = tuple(mesh.shape[name] for name in AXES)
    return jax.shard_map(
        functools.partial(on_device, sizes),
        mesh=mesh,
        in_specs=(
            P(AXES, None, None),
            P(AXES, None),
            P(AXES, None, None),
            P(AXES, None, None),
            P(AXES, None, None, None),
            P(AXES, None, None, None),
            P(AXES, None),
            P(AXES),
            P(AXES, None),
        ),
        out_specs=P(AXES, None),
        check_vma=False,
    )
```
